32 devices in a mesh: section: 4 (over x, core), tensor: 8 (over z, y).
Axes of the slice: x: 2, y: 2, z: 4, core: 2. Of those that a mesh axis runs over, the one named last changes fastest.
Arguments:
- hidden: bfloat16 [2048, 14336], P('section', 'tensor'), may hold values from -6 to 6
- down_weight: bfloat16 [4, 14336, 4096], P('section', 'tensor'), may hold values from -0.046875 to 0.046875
- down_shrink: bfloat16 [4, 14336, 256], P('section', 'tensor'), may hold values from -0.046875 to 0.046875
- down_up_factors: bfloat16 [4, 256, 4096], P('section', None, 'tensor'), may hold values from -0.5 to 0.5
- residual: bfloat16 [2048, 4096], P(('section', 'tensor')), may hold values from -6 to 6
- tenant_ids: int32 [2048], P('section'), may hold values from 0 to 3
- adapter_rank: int32 [4], replicated, may hold values from 16 to 128, as said below
- adapter_offset: int32 [4], replicated, may hold values from 0 to 224, as said below
- norm_gain: bfloat16 [4, 4096], P('section'), may hold values from 0.099609375 to 1.8984375
- qkv_weight: bfloat16 [4, 4096, 5120], P('section', None, 'tensor'), may hold values from -0.09375 to 0.09375
- qkv_shrink: bfloat16 [4, 4096, 256], P('section', None, 'tensor'), may hold values from -0.09375 to 0.09375
- qkv_expand: bfloat16 [4, 256, 5120], P('section', None, 'tensor'), may hold values from -0.5 to 0.5
Outputs:
- stream: bfloat16 [2048, 4096], P(('section', 'tensor'))
- qkv: bfloat16 [2048, 5120], P('section', 'tensor')
The draws below stay inside these ranges and needn't reach their ends.
Inputs may be any that keep to these rules, and one draw needn't show every extreme that they name: `adapter_rank`: every rank is a multiple of 16; one tenant has rank 256 // 2, the last tenant has rank 256 // 16; the ranks sum to exactly 240. `adapter_offset`: the exclusive prefix sums of adapter_rank in tenant order.
All inputs are finite; a program needn't handle non-finite values.
Results may differ from the reference program's by a relative error of at most 0.02.
Values may be sent and summed in bfloat16 or wider, within the bound.
A program may use at most 64 MiB of HBM per device.

```python
import math
import jax
import jax.numpy as jnp
import numpy as np
from jax import lax

D = 4096
FF = 14336
QKV = 5120
RANKS = 256
TENANTS = 4
ROWS = 512
SECTIONS = 4
TOTAL_ROWS = 2048
N_TENSOR = 8


def rank_table(key):
    unit = RANKS // 16
    order = jax.random.permutation(jax.random.fold_in(key, 11), 3)
    middle = jax.random.randint(jax.random.fold_in(key, 12), (), 1, 4) * unit
    slots = jnp.arange(TENANTS, dtype=jnp.int32)
    tenant_ranks = jnp.where(slots == TENANTS - 1, unit, jnp.where(slots == order[0], 8 * unit, jnp.where(slots == order[1], middle, 6 * unit - middle)))
    return tenant_ranks.astype(jnp.int32)


def draw_adapter_rank(key, part):
    tenant_ranks = rank_table(key)
    return tenant_ranks


def draw_adapter_offset(key, part):
    tenant_ranks = rank_table(key)
    return (jnp.cumsum(tenant_ranks) - tenant_ranks).astype(jnp.int32)


def set_ends(values, rng, least, top_value):
    spot = [jax.random.randint(jax.random.fold_in(rng, axis), (), 0, length) for axis, length in enumerate(values.shape)]
    longest = values.shape.index(max(values.shape))
    beside = spot[:longest] + [(spot[longest] + 1) % values.shape[longest]] + spot[longest + 1:]
    return values.at[tuple(spot)].set(least).at[tuple(beside)].set(top_value)


def level_of(stream_key, shape, split, least, top_value):
    loudness = 1.0
    for dim, blocks in split:
        heights = jax.random.uniform(jax.random.fold_in(jax.random.fold_in(stream_key, 6), dim), (blocks,), jnp.float32, least / len(split), top_value / len(split))
        loudness = loudness * jnp.repeat(jnp.exp(heights), shape[dim] // blocks).reshape((-1,) + (1,) * (len(shape) - 1 - dim))
    return loudness


def cumulative_ranks(number_of, lean):
    weights = [(1 << 20) // math.isqrt(grade ** lean) + 1 for grade in range(1, number_of + 1)]
    deviation = 1 + sum(weights) // (1 << 30)
    return np.cumsum(np.array([max(1, weight // deviation) for weight in weights]))


def ranked(rng, dims, amount, skew):
    grid = cumulative_ranks(amount, skew)
    lot = jax.random.randint(jax.random.fold_in(rng, 1), dims, 0, int(grid[amount - 1]))
    standing = jnp.searchsorted(jnp.asarray(grid, jnp.int32), lot, side="right")
    return jax.random.permutation(jax.random.fold_in(rng, 2), amount)[standing].astype(jnp.int32)


def bell_draw(rng, shape, width, most, cuts=(), kind=jnp.bfloat16):
    loudness = level_of(rng, shape, cuts, -0.22, 0.18) if cuts else 1.0
    values = jax.random.normal(rng, shape, jnp.float32) * width * loudness
    return jnp.minimum(jnp.maximum(values, -most), most).astype(kind)


def setup_inputs(seed: int = 0) -> dict:
    streams_of = jax.random.split(jax.random.key(seed), 13)
    return {
        "hidden": bell_draw(streams_of[0], (TOTAL_ROWS, FF), 1.0, 6.0, ((0, 4), (1, 8))),
        "down_weight": bell_draw(streams_of[1], (SECTIONS, FF, D), FF ** -0.5, 0.046875, ((0, 4), (1, 8))),
        "down_shrink": bell_draw(streams_of[2], (SECTIONS, FF, RANKS), FF ** -0.5, 0.046875, ((0, 4), (1, 8))),
        "down_up_factors": bell_draw(streams_of[3], (SECTIONS, RANKS, D), 128 ** -0.5, 0.5, ((0, 4), (2, 8))),
        "residual": bell_draw(streams_of[4], (TOTAL_ROWS, D), 1.0, 6.0, ((0, 32),)),
        "tenant_ids": set_ends(ranked(streams_of[5], (TOTAL_ROWS,), TENANTS, 2), jax.random.fold_in(streams_of[5], 3), 0, TENANTS - 1).astype(jnp.int32),
        "adapter_rank": draw_adapter_rank(jax.random.fold_in(streams_of[12], 71), 0),
        "adapter_offset": draw_adapter_offset(jax.random.fold_in(streams_of[12], 71), 0),
        "norm_gain": jnp.clip(1.0 + 0.18 * jax.random.normal(streams_of[8], (SECTIONS, D), jnp.float32), 0.099609375, 1.8984375).astype(jnp.bfloat16),
        "qkv_weight": bell_draw(streams_of[9], (SECTIONS, D, QKV), D ** -0.5, 0.09375, ((0, 4), (2, 8))),
        "qkv_shrink": bell_draw(streams_of[10], (SECTIONS, D, RANKS), D ** -0.5, 0.09375, ((0, 4), (2, 8))),
        "qkv_expand": bell_draw(streams_of[11], (SECTIONS, RANKS, QKV), 128 ** -0.5, 0.5, ((0, 4), (2, 8))),
    }


adapter_alpha_scale = 32.0

def table_lookup(table, tenants):
    chosen = tenants[:, None] == jnp.arange(TENANTS, dtype=jnp.int32)[None, :]
    return lax.optimization_barrier(jnp.sum(jnp.where(chosen, table[None, :], 0), axis=1)).astype(jnp.int32)

def adapter_scale(tenants, adapter_rank, adapter_offset, first_col, col_count):
    lower = table_lookup(adapter_offset, tenants)
    tenant_ranks = table_lookup(adapter_rank, tenants)
    columns = first_col + jnp.arange(col_count, dtype=jnp.int32)
    inside = (columns[None, :] >= lower[:, None]) & (columns[None, :] < (lower + tenant_ranks)[:, None])
    scaling_factor = adapter_alpha_scale / tenant_ranks.astype(jnp.float32)
    return jnp.where(inside, scaling_factor[:, None], jnp.float32(0.0))

def rounded(values):
    return lax.optimization_barrier(values.astype(jnp.bfloat16)).astype(jnp.float32)

def reference(hidden, down_weight, down_shrink, down_up_factors, residual, tenant_ids, adapter_rank, adapter_offset, norm_gain, qkv_weight, qkv_shrink, qkv_expand):
    hidden_state = hidden.reshape(SECTIONS, ROWS, FF)
    resid_st = residual.reshape(SECTIONS, ROWS, D)
    tenant_st = tenant_ids.reshape(SECTIONS, ROWS)
    block = FF // N_TENSOR

    def down_section(items):
        acts, weight, shrink, expand, resid, tenants = items

        def add_block(carry, index):
            base_acc, low_acc = carry
            start = (index * block).astype(jnp.int32)
            part_acts = lax.dynamic_slice_in_dim(acts, start, block, 1)
            part_weight = lax.dynamic_slice_in_dim(weight, start, block, 0)
            part_shrink = lax.dynamic_slice_in_dim(shrink, start, block, 0)
            base_acc = base_acc + rounded(jnp.dot(part_acts, part_weight, preferred_element_type=jnp.float32))
            low_acc = low_acc + rounded(jnp.dot(part_acts, part_shrink, preferred_element_type=jnp.float32))
            return ((base_acc, low_acc), None)
        start_carry = (jnp.zeros((ROWS, D), jnp.float32), jnp.zeros((ROWS, RANKS), jnp.float32))
        (base, low_sum), unused = lax.scan(add_block, start_carry, jnp.arange(N_TENSOR, dtype=jnp.int32))
        small = (low_sum * adapter_scale(tenants, adapter_rank, adapter_offset, 0, RANKS)).astype(jnp.bfloat16)
        output = base + jnp.dot(small, expand, preferred_element_type=jnp.float32)
        return (resid.astype(jnp.float32) + output).astype(jnp.bfloat16)
    stream = lax.map(down_section, (hidden_state, down_weight, down_shrink, down_up_factors, resid_st, tenant_st))
    arrived = jnp.roll(stream, 1, axis=0)
    arrived_ids = jnp.roll(tenant_st, 1, axis=0)

    def qkv_section(items):
        rows_in, tenants, gain, weight, shrink, expand = items
        values = rows_in.astype(jnp.float32)
        inverse = lax.rsqrt(lax.optimization_barrier(jnp.mean(values * values, axis=-1, keepdims=True)) + 1e-05)
        normed = (values * inverse * gain.astype(jnp.float32)[None, :]).astype(jnp.bfloat16)
        shrunk = jnp.dot(normed, shrink, preferred_element_type=jnp.float32)
        small = (shrunk * adapter_scale(tenants, adapter_rank, adapter_offset, 0, RANKS)).astype(jnp.bfloat16)
        output = jnp.dot(normed, weight, preferred_element_type=jnp.float32) + jnp.dot(small, expand, preferred_element_type=jnp.float32)
        return output.astype(jnp.bfloat16)
    qkv = lax.map(qkv_section, (arrived, arrived_ids, norm_gain, qkv_weight, qkv_shrink, qkv_expand))
    return (stream.reshape(TOTAL_ROWS, D), qkv.reshape(TOTAL_ROWS, QKV))
```

```python
import functools

import jax
import jax.numpy as jnp
from jax import lax
from jax.experimental import pallas as pl
from jax.experimental.pallas import tpu as pltpu
from jax.sharding import PartitionSpec as P

adapter_alpha_scale = 32.0
MESH = pl.DeviceIdType.MESH
F32 = jnp.float32
BF16 = jnp.bfloat16
CHUNK = 16
WIDE = 512


def table_lookup(table, tenants):
    chosen = tenants[:, None] == jnp.arange(table.shape[0], dtype=jnp.int32)[None, :]
    return jnp.sum(jnp.where(chosen, table[None, :], 0), axis=1)


def adapter_scale(tenants, adapter_rank, adapter_offset, first_col, col_count):
    lower = table_lookup(adapter_offset, tenants)
    tenant_ranks = table_lookup(adapter_rank, tenants)
    columns = first_col + jnp.arange(col_count, dtype=jnp.int32)
    inside = (columns[None, :] >= lower[:, None]) & (
        columns[None, :] < (lower + tenant_ranks)[:, None]
    )
    scaling_factor = adapter_alpha_scale / tenant_ranks.astype(jnp.float32)
    return jnp.where(inside, scaling_factor[:, None], jnp.float32(0.0))


def kernel(
    T,
    S,
    hidden_in,
    down_in,
    shrink_in,
    up_in,
    residual_in,
    gain_ref,
    qkv_in,
    qshrink_in,
    expand_in,
    scale_ref,
    scale_t_in,
    stream_ref,
    out_ref,
    hidden,
    down,
    shrink,
    up,
    residual,
    qkv_w,
    qshrink,
    expand,
    partial,
    lhs,
    low_mine,
    low_in,
    dlow,
    ex_out,
    ex_in,
    rs,
    arrived,
    scale_t,
    ag,
    lhs2,
    acc,
    qlow,
    qlow_all,
    load_sem,
    down_sem,
    low_ss,
    low_rs,
    dlow_ss,
    dlow_rs,
    ex_ss,
    ex_rs,
    rs_ss,
    rs_rs,
    sec_ss,
    sec_rs,
    sc_ss,
    sc_rs,
    ag_ss,
    ag_rs,
    ql_ss,
    ql_rs,
):
    rows, D = partial.shape
    share = rows // T
    half = share // 2
    n_chunk = half // CHUNK
    cols = D // T
    rc = qshrink.shape[1]
    n_wide = D // WIDE
    t = lax.axis_index("tensor")
    sec = lax.axis_index("section")
    next_sec = lax.rem(sec + 1, S)
    prev_sec = lax.rem(sec + S - 1, S)
    h = t // 2
    p = h + lax.rem(t, 2) * (T - 1 - 2 * h)

    def at_ring(q):
        q = lax.rem(q + 2 * T, T)
        u = q // (T // 2)
        return (1 - u) * 2 * q + u * (2 * (T - 1 - q) + 1)

    to = (at_ring(p + 1), at_ring(p - 1))
    step_sign = (-1, 1)

    loads = [
        pltpu.make_async_copy(a, b, load_sem.at[i])
        for i, (a, b) in enumerate(
            (
                (hidden_in, hidden),
                (shrink_in, shrink),
                (up_in, up),
                (residual_in, residual),
                (qkv_in, qkv_w),
                (qshrink_in, qshrink),
                (expand_in, expand),
            )
        )
    ]

    def down_load(j):
        at = pl.ds(pl.multiple_of(j * WIDE, WIDE), WIDE)
        return pltpu.make_async_copy(down_in.at[:, at], down.at[:, at], down_sem.at[j])

    loads[0].start()
    loads[1].start()
    for j in range(n_wide):
        down_load(j).start()
    for load in loads[2:]:
        load.start()

    barrier = pltpu.get_barrier_semaphore()
    for k in range(1, T):
        pl.semaphore_signal(
            barrier, inc=1, device_id={"tensor": lax.rem(t + k, T)}, device_id_type=MESH
        )
    for other in (next_sec, prev_sec):
        pl.semaphore_signal(
            barrier, inc=1, device_id={"section": other}, device_id_type=MESH
        )

    loads[0].wait()
    loads[1].wait()
    low_mine[...] = (
        jnp.dot(hidden[...], shrink[...], preferred_element_type=F32)
        .astype(BF16)
        .reshape(low_mine.shape)
    )
    pl.semaphore_wait(barrier, T + 1)

    def low_copy(k):
        peer = lax.rem(t + k, T)
        return pltpu.make_async_remote_copy(
            src_ref=low_mine.at[peer],
            dst_ref=low_in.at[k],
            send_sem=low_ss.at[k],
            recv_sem=low_rs.at[k],
            device_id={"tensor": peer},
            device_id_type=MESH,
        )

    def dlow_copy(k, block):
        return pltpu.make_async_remote_copy(
            src_ref=dlow.at[block],
            dst_ref=dlow.at[block],
            send_sem=dlow_ss.at[k],
            recv_sem=dlow_rs.at[k],
            device_id={"tensor": lax.rem(t + k, T)},
            device_id_type=MESH,
        )

    for k in range(1, T):
        low_copy(k).start()

    scale_copy = pltpu.make_async_remote_copy(
        src_ref=scale_t_in,
        dst_ref=scale_t,
        send_sem=sc_ss.at[0],
        recv_sem=sc_rs.at[0],
        device_id={"section": next_sec},
        device_id_type=MESH,
    )
    scale_copy.start()

    def product(j, first, second):
        at = pl.ds(pl.multiple_of(j * WIDE, WIDE), WIDE)
        got = jnp.dot(lhs[...], down[:, at], preferred_element_type=F32).astype(BF16)
        partial[pl.ds(first, share), at] = got[:share]
        partial[pl.ds(second, share), at] = got[share:]

    def pair(i):
        a = at_ring(p - 1 - i)
        last = (i + 1) // (T // 2)
        b = at_ring(p + (i + 1) * (1 - last))
        return a, b

    def row_of(block):
        return pl.multiple_of(block * share, share)

    def fill(i):
        a, b = pair(i)
        lhs[:share] = hidden[pl.ds(row_of(a), share), :]
        lhs[share:] = hidden[pl.ds(row_of(b), share), :]
        return row_of(a), row_of(b)

    my_cols = pl.ds(pl.multiple_of(t * cols, cols), cols)

    def adapter_term(block):
        return jnp.dot(dlow[block], up[...], preferred_element_type=F32)

    def add_adapter(first, count, term):
        at = pl.ds(pl.multiple_of(first, CHUNK), count)
        partial[at, my_cols] = (partial[at, my_cols].astype(F32) + term).astype(BF16)

    def run_pass(i):
        first, second = fill(i)

        @pl.loop(0, n_wide)
        def _(j):
            product(j, first, second)

    first, second = fill(0)

    def early(j):
        down_load(j).wait()
        product(j, first, second)

    pl.loop(0, n_wide // 2)(early)
    total = low_mine[t].astype(F32)
    for k in range(1, T):
        low_copy(k).wait_recv()
        total = total + low_in[k].astype(F32)
    dlow[t] = (total * scale_ref[...]).astype(BF16)
    for k in range(1, T):
        dlow_copy(k, t).start()
    pl.loop(n_wide // 2, n_wide)(early)

    def rs_copy(d, c, s, src):
        return pltpu.make_async_remote_copy(
            src_ref=src,
            dst_ref=rs.at[d, s, c],
            send_sem=rs_ss.at[d, s, c],
            recv_sem=rs_rs.at[d, s, c],
            device_id={"tensor": to[d]},
            device_id_type=MESH,
        )

    def rows_at(d, c, block):
        return pl.ds(pl.multiple_of(block * share + (d * half + c * CHUNK), CHUNK), CHUNK)

    def in_share(d, c):
        return pl.ds(d * half + c * CHUNK, CHUNK)

    lanes = [(c, d) for c in range(n_chunk) for d in range(2)]
    for c, d in lanes:
        rs_copy(d, c, 0, partial.at[rows_at(d, c, at_ring(p + step_sign[d]))]).start()

    run_pass(1)
    loads[2].wait()
    for k in range(1, T):
        dlow_copy(k, lax.rem(t + T - k, T)).wait_recv()

    def ex_copy(d):
        return pltpu.make_async_remote_copy(
            src_ref=ex_out.at[d],
            dst_ref=ex_in.at[d],
            send_sem=ex_ss.at[d],
            recv_sem=ex_rs.at[d],
            device_id={"tensor": to[1 - d]},
            device_id_type=MESH,
        )

    before, after = at_ring(p - 1), at_ring(p + 1)
    term = adapter_term(before)
    ex_out[0] = term[:half].astype(BF16)
    add_adapter(before * share + half, half, term[half:])
    term = adapter_term(after)
    ex_out[1] = term[half:].astype(BF16)
    add_adapter(after * share, half, term[:half])
    for d in range(2):
        ex_copy(d).start()

    def terms_of(i):
        a, b = pair(i)
        add_adapter(row_of(a), share, adapter_term(a))
        add_adapter(row_of(b), share, adapter_term(b))

    terms_of(1)

    @pl.loop(0, T - 2)
    def _(s):
        for c, d in lanes:
            rs_copy(d, c, s, rs.at[d, s, c]).wait_recv()
            block = at_ring(p + step_sign[d] * (s + 2))
            rs[d, s, c] = (
                rs[d, s, c].astype(F32) + partial[rows_at(d, c, block), :].astype(F32)
            ).astype(BF16)
            rs_copy(d, c, s + 1, rs.at[d, s, c]).start()

        @pl.when(s + 2 < T // 2)
        def _():
            run_pass(s + 2)
            terms_of(s + 2)

    def sec_copy(d, c):
        return pltpu.make_async_remote_copy(
            src_ref=stream_ref.at[in_share(d, c)],
            dst_ref=arrived.at[in_share(d, c)],
            send_sem=sec_ss.at[d, c],
            recv_sem=sec_rs.at[d, c],
            device_id={"section": next_sec},
            device_id_type=MESH,
        )

    def ag_copy(d, c, s, block):
        return pltpu.make_async_remote_copy(
            src_ref=ag.at[rows_at(d, c, block)],
            dst_ref=ag.at[rows_at(d, c, block)],
            send_sem=ag_ss.at[d, s, c],
            recv_sem=ag_rs.at[d, s, c],
            device_id={"tensor": to[d]},
            device_id_type=MESH,
        )

    loads[3].wait()
    for d in range(2):
        ex_copy(d).wait_recv()
    for c, d in lanes:
        s = T - 2
        rs_copy(d, c, s, rs.at[d, s, c]).wait_recv()
        at = in_share(d, c)
        mine = rows_at(d, c, t)
        total = rs[d, s, c].astype(F32) + partial[mine, :].astype(F32)
        rs[d, s, c] = total.astype(BF16)
        stream_ref[at, :] = (total + residual[at, :].astype(F32)).astype(BF16)
        sender_cols = pl.ds(pl.multiple_of(at_ring(p - step_sign[d]) * cols, cols), cols)
        stream_ref[at, sender_cols] = (
            rs[d, s, c, :, sender_cols].astype(F32)
            + ex_in[d, pl.ds(c * CHUNK, CHUNK), :].astype(F32)
            + residual[at, sender_cols].astype(F32)
        ).astype(BF16)
        sec_copy(d, c).start()
    for c, d in lanes:
        at = in_share(d, c)
        sec_copy(d, c).wait_recv()
        values = arrived[at, :].astype(F32)
        inverse = lax.rsqrt(jnp.mean(values * values, axis=-1, keepdims=True) + 1e-05)
        ag[rows_at(d, c, t), :] = (values * inverse * gain_ref[...].astype(F32)).astype(BF16)
        ag_copy(d, c, 0, t).start()

    for load in loads[4:]:
        load.wait()
    qlow[...] = jnp.zeros_like(qlow)

    def multiply(a, b):
        at_a = pl.ds(pl.multiple_of(a * share, half), half)
        at_b = pl.ds(pl.multiple_of(b * share + half, half), half)
        lhs2[:half] = ag[at_a, :]
        lhs2[half:] = ag[at_b, :]
        low = jnp.dot(lhs2[...], qshrink[...], preferred_element_type=F32)
        qlow[at_a, :rc] = low[:half]
        qlow[at_b, :rc] = low[half:]

        def rest():
            got = jnp.dot(lhs2[...], qkv_w[...], preferred_element_type=F32)
            acc[at_a, :] = got[:half]
            acc[at_b, :] = got[half:]

        return rest

    multiply(t, t)()

    def gather_step(s, forward):
        for c, d in lanes:
            block = at_ring(p + step_sign[d] * (s + 1))
            ag_copy(d, c, s, block).wait_recv()
            if forward:
                ag_copy(d, c, s + 1, block).start()
        return multiply(at_ring(p - s - 1), at_ring(p + s + 1))

    @pl.loop(0, T - 2)
    def _(s):
        gather_step(s, True)()

    rest = gather_step(T - 2, False)
    scale_copy.wait()
    qlow_all[t] = (qlow[...].T[:rc] * scale_t[...]).astype(BF16)

    def ql_copy(k, block):
        return pltpu.make_async_remote_copy(
            src_ref=qlow_all.at[block],
            dst_ref=qlow_all.at[block],
            send_sem=ql_ss.at[k],
            recv_sem=ql_rs.at[k],
            device_id={"tensor": lax.rem(t + k, T)},
            device_id_type=MESH,
        )

    for k in range(1, T):
        ql_copy(k, t).start()
    rest()
    for k in range(1, T):
        ql_copy(k, lax.rem(t + T - k, T)).wait_recv()
    small = qlow_all[...].reshape(T * rc, rows)
    added = lax.dot_general(
        small, expand[...], (((0,), (0,)), ((), ())), preferred_element_type=F32
    )
    out_ref[...] = (acc[...] + added).astype(BF16)

    for k in range(1, T):
        low_copy(k).wait_send()
        dlow_copy(k, t).wait_send()
        ql_copy(k, t).wait_send()
    for d in range(2):
        ex_copy(d).wait_send()
        for c in range(n_chunk):
            sec_copy(d, c).wait_send()

            @pl.loop(0, T - 1)
            def _(s):
                rs_copy(d, c, s, rs.at[d, s, c]).wait_send()
                ag_copy(d, c, s, t).wait_send()


def per_device(
    T,
    S,
    hidden,
    down_weight,
    down_shrink,
    down_up_factors,
    residual,
    tenant_ids,
    adapter_rank,
    adapter_offset,
    norm_gain,
    qkv_weight,
    qkv_shrink,
    qkv_expand,
):
    rows, K = hidden.shape
    D = residual.shape[1]
    share = rows // T
    half = share // 2
    n_chunk = half // CHUNK
    R = down_shrink.shape[2]
    Q = qkv_weight.shape[2]
    rc = qkv_shrink.shape[2]
    cols = down_up_factors.shape[2]
    t = lax.axis_index("tensor")
    my_tenants = lax.dynamic_slice_in_dim(tenant_ids, t * share, share, 0)
    scale = adapter_scale(my_tenants, adapter_rank, adapter_offset, 0, R)
    scale_t = adapter_scale(tenant_ids, adapter_rank, adapter_offset, t * rc, rc).T

    any_spec = pl.BlockSpec(memory_space=pl.ANY)
    vmem = pl.BlockSpec(memory_space=pltpu.VMEM)
    dma = pltpu.SemaphoreType.DMA
    return pl.pallas_call(
        functools.partial(kernel, T, S),
        out_shape=(
            jax.ShapeDtypeStruct((share, D), BF16),
            jax.ShapeDtypeStruct((rows, Q), BF16),
        ),
        in_specs=[any_spec] * 5 + [vmem] + [any_spec] * 3 + [vmem] * 2,
        out_specs=(vmem, vmem),
        scratch_shapes=[
            pltpu.VMEM((rows, K), BF16),
            pltpu.VMEM((K, D), BF16),
            pltpu.VMEM((K, R), BF16),
            pltpu.VMEM((R, cols), BF16),
            pltpu.VMEM((share, D), BF16),
            pltpu.VMEM((D, Q), BF16),
            pltpu.VMEM((D, rc), BF16),
            pltpu.VMEM((R, Q), BF16),
            pltpu.VMEM((rows, D), BF16),
            pltpu.VMEM((2 * share, K), BF16),
            pltpu.VMEM((T, share, R), BF16),
            pltpu.VMEM((T, share, R), BF16),
            pltpu.VMEM((T, share, R), BF16),
            pltpu.VMEM((2, half, cols), BF16),
            pltpu.VMEM((2, half, cols), BF16),
            pltpu.VMEM((2, T - 1, n_chunk, CHUNK, D), BF16),
            pltpu.VMEM((share, D), BF16),
            pltpu.VMEM((rc, rows), F32),
            pltpu.VMEM((rows, D), BF16),
            pltpu.VMEM((share, D), BF16),
            pltpu.VMEM((rows, Q), F32),
            pltpu.VMEM((rows, 128), F32),
            pltpu.VMEM((T, rc, rows), BF16),
            dma((7,)),
            dma((D // WIDE,)),
            dma((T,)),
            dma((T,)),
            dma((T,)),
            dma((T,)),
            dma((2,)),
            dma((2,)),
            dma((2, T - 1, n_chunk)),
            dma((2, T - 1, n_chunk)),
            dma((2, n_chunk)),
            dma((2, n_chunk)),
            dma((1,)),
            dma((1,)),
            dma((2, T - 1, n_chunk)),
            dma((2, T - 1, n_chunk)),
            dma((T,)),
            dma((T,)),
        ],
        compiler_params=pltpu.CompilerParams(
            collective_id=0, has_side_effects=True, vmem_limit_bytes=60 * 1024 * 1024
        ),
        name="relay_boundary",
    )(
        hidden,
        down_weight[0],
        down_shrink[0],
        down_up_factors[0],
        residual,
        norm_gain,
        qkv_weight[0],
        qkv_shrink[0],
        qkv_expand[0],
        scale,
        scale_t,
    )


def solution(mesh):
    in_specs = (
        P("section", "tensor"),
        P("section", "tensor", None),
        P("section", "tensor", None),
        P("section", None, "tensor"),
        P(("section", "tensor"), None),
        P("section"),
        P(),
        P(),
        P("section", None),
        P("section", None, "tensor"),
        P("section", None, "tensor"),
        P("section", None, "tensor"),
    )
    out_specs = (P(("section", "tensor"), None), P("section", "tensor"))
    body = functools.partial(per_device, mesh.shape["tensor"], mesh.shape["section"])
    return jax.shard_map(
        body, mesh=mesh, in_specs=in_specs, out_specs=out_specs, check_vma=False
    )
```

```python
import functools

import jax
import jax.numpy as jnp
from jax import lax
from jax.experimental import pallas as pl
from jax.experimental.pallas import tpu as pltpu
from jax.sharding import PartitionSpec as P

adapter_alpha_scale = 32.0
MESH = pl.DeviceIdType.MESH
F32 = jnp.float32
BF16 = jnp.bfloat16
CHUNK = 16
WIDE = 512


def kernel(
    T,
    S,
    hidden_in,
    down_in,
    shrink_in,
    up_in,
    residual_in,
    gain_ref,
    qkv_in,
    qshrink_in,
    expand_in,
    ids_ref,
    rank_ref,
    offset_ref,
    stream_ref,
    out_ref,
    hidden,
    down,
    shrink,
    up,
    residual,
    qkv_w,
    qshrink,
    expand,
    partial,
    lhs,
    low_mine,
    low_in,
    dlow,
    ex_out,
    ex_in,
    rs,
    arrived,
    scale_t,
    scale_all,
    scale_rows,
    ag,
    lhs2,
    acc,
    qlow,
    qlow_all,
    load_sem,
    down_sem,
    low_ss,
    low_rs,
    dlow_ss,
    dlow_rs,
    ex_ss,
    ex_rs,
    rs_ss,
    rs_rs,
    sec_ss,
    sec_rs,
    sc_ss,
    sc_rs,
    ag_ss,
    ag_rs,
    ql_ss,
    ql_rs,
):
    rows, D = partial.shape
    share = rows // T
    half = share // 2
    n_chunk = half // CHUNK
    cols = D // T
    rc = qshrink.shape[0]
    n_wide = D // WIDE
    t = lax.axis_index("tensor")
    sec = lax.axis_index("section")
    next_sec = lax.rem(sec + 1, S)
    prev_sec = lax.rem(sec + S - 1, S)
    h = t // 2
    p = h + lax.rem(t, 2) * (T - 1 - 2 * h)

    def at_ring(q):
        q = lax.rem(q + 2 * T, T)
        u = q // (T // 2)
        return (1 - u) * 2 * q + u * (2 * (T - 1 - q) + 1)

    to = (at_ring(p + 1), at_ring(p - 1))
    sign = (1, -1)
    far = T // 2
    all_chunks = 2 * n_chunk
    first_half, second_half = range(n_chunk), range(n_chunk, all_chunks)
    mixed = [c for pair_of in zip(second_half, first_half) for c in pair_of]
    swapped = [c for pair_of in zip(first_half, second_half) for c in pair_of]
    whole_way = (first_half, second_half)
    one_less = (second_half, first_half)

    loads = [
        pltpu.make_async_copy(a, b, load_sem.at[i])
        for i, (a, b) in enumerate(
            (
                (hidden_in, hidden),
                (shrink_in, shrink),
                (up_in, up),
                (residual_in, residual),
                (qkv_in, qkv_w),
                (qshrink_in, qshrink),
                (expand_in, expand),
            )
        )
    ]

    def down_load(j):
        at = pl.ds(pl.multiple_of(j * WIDE, WIDE), WIDE)
        return pltpu.make_async_copy(down_in.at[:, at], down.at[:, at], down_sem.at[j])

    loads[0].start()
    loads[1].start()
    for j in range(n_wide):
        down_load(j).start()
    for load in loads[2:]:
        load.start()

    barrier = pltpu.get_barrier_semaphore()
    for k in range(1, T):
        pl.semaphore_signal(
            barrier, inc=1, device_id={"tensor": lax.rem(t + k, T)}, device_id_type=MESH
        )
    for other in (next_sec, prev_sec):
        pl.semaphore_signal(
            barrier, inc=1, device_id={"section": other}, device_id_type=MESH
        )

    ids = ids_ref[...]
    lower = jnp.zeros_like(ids)
    ranks = jnp.zeros_like(ids)
    for k in range(rank_ref.shape[0]):
        lower = lower + jnp.where(ids == k, offset_ref[k], 0)
        ranks = ranks + jnp.where(ids == k, rank_ref[k], 0)
    column = lax.broadcasted_iota(jnp.int32, scale_all.shape, 0)
    inside = (column >= lower) & (column < lower + ranks)
    scale_all[...] = jnp.where(inside, adapter_alpha_scale / ranks.astype(F32), 0.0)
    scale_rows[...] = scale_all[...].T

    loads[0].wait()
    loads[1].wait()
    low_mine[...] = (
        jnp.dot(hidden[...], shrink[...], preferred_element_type=F32)
        .astype(BF16)
        .reshape(low_mine.shape)
    )
    pl.semaphore_wait(barrier, T + 1)

    def low_copy(k):
        peer = lax.rem(t + k, T)
        return pltpu.make_async_remote_copy(
            src_ref=low_mine.at[peer],
            dst_ref=low_in.at[k],
            send_sem=low_ss.at[k],
            recv_sem=low_rs.at[k],
            device_id={"tensor": peer},
            device_id_type=MESH,
        )

    def dlow_copy(k, block):
        return pltpu.make_async_remote_copy(
            src_ref=dlow.at[block],
            dst_ref=dlow.at[block],
            send_sem=dlow_ss.at[k],
            recv_sem=dlow_rs.at[k],
            device_id={"tensor": lax.rem(t + k, T)},
            device_id_type=MESH,
        )

    for k in range(1, T):
        low_copy(k).start()

    scale_copy = pltpu.make_async_remote_copy(
        src_ref=scale_all.at[pl.ds(pl.multiple_of(t * rc, rc), rc)],
        dst_ref=scale_t,
        send_sem=sc_ss.at[0],
        recv_sem=sc_rs.at[0],
        device_id={"section": next_sec},
        device_id_type=MESH,
    )
    scale_copy.start()

    def product(j, first, second):
        at = pl.ds(pl.multiple_of(j * WIDE, WIDE), WIDE)
        got = jnp.dot(lhs[...], down[:, at], preferred_element_type=F32).astype(BF16)
        partial[pl.ds(first, share), at] = got[:share]
        partial[pl.ds(second, share), at] = got[share:]

    def pair(i):
        return at_ring(p + far - i), (t if i == 0 else at_ring(p - far + i))

    def row_of(block):
        return pl.multiple_of(block * share, share)

    def fill(i):
        a, b = pair(i)
        lhs[:share] = hidden[pl.ds(row_of(a), share), :]
        lhs[share:] = hidden[pl.ds(row_of(b), share), :]
        return row_of(a), row_of(b)

    my_cols = pl.ds(pl.multiple_of(t * cols, cols), cols)

    def adapter_term(block):
        return jnp.dot(dlow[block], up[...], preferred_element_type=F32)

    def add_adapter(first, count, term):
        at = pl.ds(pl.multiple_of(first, CHUNK), count)
        partial[at, my_cols] = (partial[at, my_cols].astype(F32) + term).astype(BF16)

    def run_pass(i):
        first, second = fill(i)

        @pl.loop(0, n_wide)
        def _(j):
            product(j, first, second)

    first, second = fill(0)

    def early(j):
        down_load(j).wait()
        product(j, first, second)

    pl.loop(0, n_wide // 2)(early)
    total = low_mine[t].astype(F32)
    for k in range(1, T):
        low_copy(k).wait_recv()
        total = total + low_in[k].astype(F32)
    dlow[t] = (total * scale_rows[pl.ds(row_of(t), share), :]).astype(BF16)
    for k in range(1, T):
        dlow_copy(k, t).start()
    pl.loop(n_wide // 2, n_wide)(early)

    def rs_copy(d, c, k, src):
        return pltpu.make_async_remote_copy(
            src_ref=src,
            dst_ref=rs.at[d, k - 1, c],
            send_sem=rs_ss.at[d, k - 1, c],
            recv_sem=rs_rs.at[d, k - 1, c],
            device_id={"tensor": to[d]},
            device_id_type=MESH,
        )

    def rows_at(c, block):
        return pl.ds(pl.multiple_of(block * share + c * CHUNK, CHUNK), CHUNK)

    def in_share(c):
        return pl.ds(c * CHUNK, CHUNK)

    def begin(d, c, k):
        rs_copy(d, c, k, partial.at[rows_at(c, at_ring(p + sign[d] * k))]).start()

    def ex_copy(d):
        return pltpu.make_async_remote_copy(
            src_ref=ex_out.at[d],
            dst_ref=ex_in.at[d],
            send_sem=ex_ss.at[d],
            recv_sem=ex_rs.at[d],
            device_id={"tensor": to[d]},
            device_id_type=MESH,
        )

    def pass_on(d, c, k):
        slot = rs.at[d, k, c]
        rs_copy(d, c, k + 1, slot).wait_recv()
        here = rows_at(c, at_ring(p + sign[d] * k))
        if k + 1 == far:
            sender_cols = pl.ds(pl.multiple_of(at_ring(p - sign[d]) * cols, cols), cols)
            late = ex_in[d, pl.ds((c - d * n_chunk) * CHUNK, CHUNK), :].astype(F32)
            slot[:, sender_cols] = (slot[:, sender_cols].astype(F32) + late).astype(BF16)
        slot[...] = (slot[...].astype(F32) + partial[here, :].astype(F32)).astype(BF16)
        rs_copy(d, c, k, slot).start()

    for i in range(n_chunk):
        for d in range(2):
            begin(d, whole_way[d][i], far)

    run_pass(1)
    loads[2].wait()
    for k in range(1, T):
        dlow_copy(k, lax.rem(t + T - k, T)).wait_recv()

    def add_terms(block):
        term = jnp.dot(dlow[block], up[...], preferred_element_type=F32)
        at = pl.ds(row_of(block), share)
        partial[at, my_cols] = (partial[at, my_cols].astype(F32) + term).astype(BF16)

    term = jnp.dot(dlow[at_ring(p + far)], up[...], preferred_element_type=F32)
    ex_out[0] = term[:half].astype(BF16)
    ex_out[1] = term[half:].astype(BF16)
    for d in range(2):
        ex_copy(d).start()

    def terms_of(i):
        for block in pair(i):
            add_terms(block)

    terms_of(1)
    for i in range(n_chunk):
        for d in range(2):
            begin(d, one_less[d][i], far - 1)
    if far > 2:
        run_pass(2)
        terms_of(2)
    for d in range(2):
        ex_copy(d).wait_recv()
    for i in range(n_chunk):
        for d in range(2):
            pass_on(d, whole_way[d][i], far - 1)
    for k in range(far - 2, 0, -1):
        if far - k > 2:
            run_pass(far - k)
            terms_of(far - k)
        for i in range(all_chunks):
            for d in range(2):
                pass_on(d, (mixed if d == 0 or k == 1 else swapped)[i], k)
    add_terms(t)

    def sec_copy(c):
        return pltpu.make_async_remote_copy(
            src_ref=stream_ref.at[in_share(c)],
            dst_ref=arrived.at[in_share(c)],
            send_sem=sec_ss.at[c],
            recv_sem=sec_rs.at[c],
            device_id={"section": next_sec},
            device_id_type=MESH,
        )

    def ag_copy(d, c, hop, block):
        return pltpu.make_async_remote_copy(
            src_ref=ag.at[rows_at(c, block)],
            dst_ref=ag.at[rows_at(c, block)],
            send_sem=ag_ss.at[d, hop, c],
            recv_sem=ag_rs.at[d, hop, c],
            device_id={"tensor": to[d]},
            device_id_type=MESH,
        )

    loads[3].wait()

    def finish(c):
        at = in_share(c)
        total = partial[rows_at(c, t), :].astype(F32) + residual[at, :].astype(F32)
        for d in range(2):
            rs_copy(d, c, 1, rs.at[d, 0, c]).wait_recv()
            total = total + rs[d, 0, c].astype(F32)
        stream_ref[at, :] = total.astype(BF16)
        sec_copy(c).start()

    def normalise(c):
        sec_copy(c).wait_recv()
        values = arrived[in_share(c), :].astype(F32)
        inverse = lax.rsqrt(jnp.mean(values * values, axis=-1, keepdims=True) + 1e-05)
        ag[rows_at(c, t), :] = (values * inverse * gain_ref[...].astype(F32)).astype(BF16)
        for d in range(2):
            ag_copy(d, c, 0, t).start()

    for i, c in enumerate(mixed):
        finish(c)
        if i:
            normalise(mixed[i - 1])
    normalise(mixed[-1])

    for load in loads[4:]:
        load.wait()
    qlow[...] = jnp.zeros_like(qlow)

    NT = (((1,), (1,)), ((), ()))

    def multiply(blocks):
        count = len(blocks) * share
        for i, block in enumerate(blocks):
            lhs2[pl.ds(i * share, share), :] = ag[pl.ds(row_of(block), share), :]
        low = lax.dot_general(lhs2[:count], qshrink[...], NT, preferred_element_type=F32)
        for i, block in enumerate(blocks):
            qlow[pl.ds(row_of(block), share), :rc] = low[i * share : (i + 1) * share]

        def rest():
            got = jnp.dot(lhs2[:count], qkv_w[...], preferred_element_type=F32)
            for i, block in enumerate(blocks):
                acc[pl.ds(row_of(block), share), :] = got[i * share : (i + 1) * share]

        return rest

    multiply([t])()
    for hop in range(far - 1):
        for c in mixed:
            for d in range(2):
                block = at_ring(p - sign[d] * (hop + 1))
                ag_copy(d, c, hop, block).wait_recv()
                if hop + 1 < far - 1 or c in whole_way[d]:
                    ag_copy(d, c, hop + 1, block).start()
        multiply([at_ring(p - hop - 1), at_ring(p + hop + 1)])()
    opposite = at_ring(p + far)
    for d in range(2):
        for c in whole_way[d]:
            ag_copy(d, c, far - 1, opposite).wait_recv()
    rest = multiply([opposite])
    scale_copy.wait()
    qlow_all[t] = (qlow[...].T[:rc] * scale_t[...]).astype(BF16)

    def ql_copy(k, block):
        return pltpu.make_async_remote_copy(
            src_ref=qlow_all.at[block],
            dst_ref=qlow_all.at[block],
            send_sem=ql_ss.at[k],
            recv_sem=ql_rs.at[k],
            device_id={"tensor": lax.rem(t + k, T)},
            device_id_type=MESH,
        )

    for k in range(1, T):
        ql_copy(k, t).start()
    rest()
    for k in range(1, T):
        ql_copy(k, lax.rem(t + T - k, T)).wait_recv()
    small = qlow_all[...].reshape(T * rc, rows)
    added = lax.dot_general(
        small, expand[...], (((0,), (0,)), ((), ())), preferred_element_type=F32
    )
    out_ref[...] = (acc[...] + added).astype(BF16)

    for k in range(1, T):
        low_copy(k).wait_send()
        dlow_copy(k, t).wait_send()
        ql_copy(k, t).wait_send()
    for c in range(all_chunks):
        sec_copy(c).wait_send()
    for d in range(2):
        ex_copy(d).wait_send()
        for c in range(all_chunks):
            for k in range(far if c in whole_way[d] else far - 1):
                rs_copy(d, c, k + 1, rs.at[d, k, c]).wait_send()
                ag_copy(d, c, k, t).wait_send()


def copy_out(stream_in, out_in, stream_ref, out_ref, sem):
    copies = [
        pltpu.make_async_copy(stream_in, stream_ref, sem.at[0]),
        pltpu.make_async_copy(out_in, out_ref, sem.at[1]),
    ]
    for copy in copies:
        copy.start()
    for copy in copies:
        copy.wait()


def per_device(
    T,
    S,
    hidden,
    down_weight,
    down_shrink,
    down_up_factors,
    residual,
    tenant_ids,
    adapter_rank,
    adapter_offset,
    norm_gain,
    qkv_weight,
    qkv_shrink,
    qkv_expand,
):
    rows, K = hidden.shape
    D = residual.shape[1]
    share = rows // T
    half = share // 2
    R = down_shrink.shape[2]
    Q = qkv_weight.shape[2]
    rc = qkv_shrink.shape[2]
    cols = down_up_factors.shape[2]
    any_spec = pl.BlockSpec(memory_space=pl.ANY)
    vmem = pl.BlockSpec(memory_space=pltpu.VMEM)
    dma = pltpu.SemaphoreType.DMA
    smem = pl.BlockSpec(memory_space=pltpu.SMEM)
    outs = pl.pallas_call(
        functools.partial(kernel, T, S),
        out_shape=(
            pltpu.VMEM((share, D), BF16),
            pltpu.VMEM((rows, Q), BF16),
        ),
        in_specs=[any_spec] * 5 + [vmem] + [any_spec] * 3 + [vmem, smem, smem],
        out_specs=(vmem, vmem),
        scratch_shapes=[
            pltpu.VMEM((rows, K), BF16),
            pltpu.VMEM((K, D), BF16),
            pltpu.VMEM((K, R), BF16),
            pltpu.VMEM((R, cols), BF16),
            pltpu.VMEM((share, D), BF16),
            pltpu.VMEM((D, Q), BF16),
            pltpu.VMEM((rc, D), BF16),
            pltpu.VMEM((R, Q), BF16),
            pltpu.VMEM((rows, D), BF16),
            pltpu.VMEM((2 * share, K), BF16),
            pltpu.VMEM((T, share, R), BF16),
            pltpu.VMEM((T, share, R), BF16),
            pltpu.VMEM((T, share, R), BF16),
            pltpu.VMEM((2, half, cols), BF16),
            pltpu.VMEM((2, half, cols), BF16),
            pltpu.VMEM((2, T // 2, share // CHUNK, CHUNK, D), BF16),
            pltpu.VMEM((share, D), BF16),
            pltpu.VMEM((rc, rows), F32),
            pltpu.VMEM((R, rows), F32),
            pltpu.VMEM((rows, R), F32),
            pltpu.VMEM((rows, D), BF16),
            pltpu.VMEM((2 * share, D), BF16),
            pltpu.VMEM((rows, Q), F32),
            pltpu.VMEM((rows, 128), F32),
            pltpu.VMEM((T, rc, rows), BF16),
            dma((7,)),
            dma((D // WIDE,)),
            dma((T,)),
            dma((T,)),
            dma((T,)),
            dma((T,)),
            dma((2,)),
            dma((2,)),
            dma((2, T // 2, share // CHUNK)),
            dma((2, T // 2, share // CHUNK)),
            dma((share // CHUNK,)),
            dma((share // CHUNK,)),
            dma((1,)),
            dma((1,)),
            dma((2, T // 2, share // CHUNK)),
            dma((2, T // 2, share // CHUNK)),
            dma((T,)),
            dma((T,)),
        ],
        compiler_params=pltpu.CompilerParams(
            collective_id=0, has_side_effects=True, vmem_limit_bytes=61 * 1024 * 1024
        ),
        name="relay_boundary",
    )(
        hidden,
        down_weight[0],
        down_shrink[0],
        down_up_factors[0],
        residual,
        norm_gain,
        qkv_weight[0],
        qkv_shrink[0].T,
        qkv_expand[0],
        tenant_ids.reshape(1, rows),
        adapter_rank,
        adapter_offset,
    )
    return pl.pallas_call(
        copy_out,
        out_shape=tuple(jax.ShapeDtypeStruct(o.shape, o.dtype) for o in outs),
        in_specs=[vmem] * 2,
        out_specs=(any_spec, any_spec),
        scratch_shapes=[dma((2,))],
        name="copy_out",
    )(*outs)


def solution(mesh):
    in_specs = (
        P("section", "tensor"),
        P("section", "tensor", None),
        P("section", "tensor", None),
        P("section", None, "tensor"),
        P(("section", "tensor"), None),
        P("section"),
        P(),
        P(),
        P("section", None),
        P("section", None, "tensor"),
        P("section", None, "tensor"),
        P("section", None, "tensor"),
    )
    out_specs = (P(("section", "tensor"), None), P("section", "tensor"))
    body = functools.partial(per_device, mesh.shape["tensor"], mesh.shape["section"])
    return jax.shard_map(
        body, mesh=mesh, in_specs=in_specs, out_specs=out_specs, check_vma=False
    )
```

```python
import functools

import jax
import jax.numpy as jnp
from jax import lax
from jax.experimental import pallas as pl
from jax.experimental.pallas import tpu as pltpu
from jax.sharding import PartitionSpec as P

adapter_alpha_scale = 32.0
MESH = pl.DeviceIdType.MESH
F32 = jnp.float32
BF16 = jnp.bfloat16
CHUNK = 16
WIDE = 512


def kernel(
    T,
    S,
    hidden_in,
    down_in,
    shrink_in,
    up_in,
    residual_in,
    gain_ref,
    qkv_in,
    qshrink_in,
    expand_in,
    ids_ref,
    rank_ref,
    offset_ref,
    stream_ref,
    out_ref,
    hidden,
    down,
    shrink,
    up,
    residual,
    qkv_w,
    qshrink,
    expand,
    partial,
    lhs,
    low_mine,
    low_in,
    dlow,
    ex_out,
    ex_in,
    rs,
    arrived,
    scale_t,
    scale_all,
    scale_rows,
    ag,
    lhs2,
    acc,
    qlow,
    qlow_all,
    load_sem,
    down_sem,
    low_ss,
    low_rs,
    dlow_ss,
    dlow_rs,
    ex_ss,
    ex_rs,
    rs_ss,
    rs_rs,
    sec_ss,
    sec_rs,
    sc_ss,
    sc_rs,
    ag_ss,
    ag_rs,
    ql_ss,
    ql_rs,
):
    rows, D = partial.shape
    share = rows // T
    half = share // 2
    n_chunk = half // CHUNK
    cols = D // T
    rc = qshrink.shape[0]
    n_wide = D // WIDE
    t = lax.axis_index("tensor")
    sec = lax.axis_index("section")
    next_sec = lax.rem(sec + 1, S)
    prev_sec = lax.rem(sec + S - 1, S)
    h = t // 2
    p = h + lax.rem(t, 2) * (T - 1 - 2 * h)

    def at_ring(q):
        q = lax.rem(q + 2 * T, T)
        u = q // (T // 2)
        return (1 - u) * 2 * q + u * (2 * (T - 1 - q) + 1)

    to = (at_ring(p + 1), at_ring(p - 1))
    sign = (1, -1)
    far = T // 2
    all_chunks = 2 * n_chunk
    first_half, second_half = range(n_chunk), range(n_chunk, all_chunks)
    mixed = [c for pair_of in zip(second_half, first_half) for c in pair_of]
    swapped = [c for pair_of in zip(first_half, second_half) for c in pair_of]
    whole_way = (first_half, second_half)
    one_less = (second_half, first_half)

    def pieces(source, target, sem, count):
        size = target.shape[0] // count
        return [
            pltpu.make_async_copy(
                source.at[pl.ds(i * size, size)], target.at[pl.ds(i * size, size)], sem
            )
            for i in range(count)
        ]

    wide_k = down.shape[0] // 4

    def down_load(j, first, size):
        at = pl.ds(pl.multiple_of(j * WIDE, WIDE), WIDE)
        part = pl.ds(first, size)
        return pltpu.make_async_copy(down_in.at[part, at], down.at[part, at], down_sem.at[j])

    arrays = (
        (hidden_in, hidden, 8),
        (shrink_in, shrink, 4),
        (up_in, up, 1),
        (residual_in, residual, 1),
        (qkv_in, qkv_w, 4),
        (qshrink_in, qshrink, 1),
        (expand_in, expand, 1),
    )
    loads = [pltpu.make_async_copy(x, y, load_sem.at[i]) for i, (x, y, n) in enumerate(arrays)]
    parts = [pieces(x, y, load_sem.at[i], n) for i, (x, y, n) in enumerate(arrays)]
    for copy in parts[0] + parts[1]:
        copy.start()
    for j in range(n_wide):
        for i in range(4):
            down_load(j, i * wide_k, wide_k).start()
    for copies in parts[2:]:
        for copy in copies:
            copy.start()

    barrier = pltpu.get_barrier_semaphore()
    for k in range(1, T):
        pl.semaphore_signal(
            barrier, inc=1, device_id={"tensor": lax.rem(t + k, T)}, device_id_type=MESH
        )
    for other in (next_sec, prev_sec):
        pl.semaphore_signal(
            barrier, inc=1, device_id={"section": other}, device_id_type=MESH
        )

    ids = ids_ref[...]
    lower = jnp.zeros_like(ids)
    ranks = jnp.zeros_like(ids)
    for k in range(rank_ref.shape[0]):
        lower = lower + jnp.where(ids == k, offset_ref[k], 0)
        ranks = ranks + jnp.where(ids == k, rank_ref[k], 0)
    column = lax.broadcasted_iota(jnp.int32, scale_all.shape, 0)
    inside = (column >= lower) & (column < lower + ranks)
    scale_all[...] = jnp.where(inside, adapter_alpha_scale / ranks.astype(F32), 0.0)
    scale_rows[...] = scale_all[...].T

    loads[0].wait()
    loads[1].wait()
    low_mine[...] = (
        jnp.dot(hidden[...], shrink[...], preferred_element_type=F32)
        .astype(BF16)
        .reshape(low_mine.shape)
    )
    pl.semaphore_wait(barrier, T + 1)

    def low_copy(k):
        peer = lax.rem(t + k, T)
        return pltpu.make_async_remote_copy(
            src_ref=low_mine.at[peer],
            dst_ref=low_in.at[k],
            send_sem=low_ss.at[k],
            recv_sem=low_rs.at[k],
            device_id={"tensor": peer},
            device_id_type=MESH,
        )

    def dlow_copy(k, block):
        return pltpu.make_async_remote_copy(
            src_ref=dlow.at[block],
            dst_ref=dlow.at[block],
            send_sem=dlow_ss.at[k],
            recv_sem=dlow_rs.at[k],
            device_id={"tensor": lax.rem(t + k, T)},
            device_id_type=MESH,
        )

    for k in range(1, T):
        low_copy(k).start()

    scale_copy = pltpu.make_async_remote_copy(
        src_ref=scale_all.at[pl.ds(pl.multiple_of(t * rc, rc), rc)],
        dst_ref=scale_t,
        send_sem=sc_ss.at[0],
        recv_sem=sc_rs.at[0],
        device_id={"section": next_sec},
        device_id_type=MESH,
    )
    scale_copy.start()

    def product(j, first, second):
        at = pl.ds(pl.multiple_of(j * WIDE, WIDE), WIDE)
        got = jnp.dot(lhs[...], down[:, at], preferred_element_type=F32).astype(BF16)
        partial[pl.ds(first, share), at] = got[:share]
        partial[pl.ds(second, share), at] = got[share:]

    def pair(i):
        return at_ring(p + far - i), (t if i == 0 else at_ring(p - far + i))

    def row_of(block):
        return pl.multiple_of(block * share, share)

    def fill(i):
        a, b = pair(i)
        lhs[:share] = hidden[pl.ds(row_of(a), share), :]
        lhs[share:] = hidden[pl.ds(row_of(b), share), :]
        return row_of(a), row_of(b)

    my_cols = pl.ds(pl.multiple_of(t * cols, cols), cols)

    def adapter_term(block):
        return jnp.dot(dlow[block], up[...], preferred_element_type=F32)

    def add_adapter(first, count, term):
        at = pl.ds(pl.multiple_of(first, CHUNK), count)
        partial[at, my_cols] = (partial[at, my_cols].astype(F32) + term).astype(BF16)

    def run_pass(i):
        first, second = fill(i)

        @pl.loop(0, n_wide)
        def _(j):
            product(j, first, second)

    def rows_at(c, block):
        return pl.ds(pl.multiple_of(block * share + c * CHUNK, CHUNK), CHUNK)

    first, second = fill(0)

    def early(j):
        down_load(j, 0, down.shape[0]).wait()
        product(j, first, second)

    pl.loop(0, n_wide // 2)(early)
    total = low_mine[t].astype(F32)
    for k in range(1, T):
        low_copy(k).wait_recv()
        total = total + low_in[k].astype(F32)
    dlow[t] = (total * scale_rows[pl.ds(row_of(t), share), :]).astype(BF16)
    for k in range(1, T):
        dlow_copy(k, t).start()
    pl.loop(n_wide // 2, n_wide)(early)

    def rs_copy(d, c, k, src):
        return pltpu.make_async_remote_copy(
            src_ref=src,
            dst_ref=rs.at[d, k - 1, c],
            send_sem=rs_ss.at[d, k - 1, c],
            recv_sem=rs_rs.at[d, k - 1, c],
            device_id={"tensor": to[d]},
            device_id_type=MESH,
        )

    def in_share(c):
        return pl.ds(c * CHUNK, CHUNK)

    def begin(d, c, k):
        rs_copy(d, c, k, partial.at[rows_at(c, at_ring(p + sign[d] * k))]).start()

    def ex_copy(d):
        return pltpu.make_async_remote_copy(
            src_ref=ex_out.at[d],
            dst_ref=ex_in.at[d],
            send_sem=ex_ss.at[d],
            recv_sem=ex_rs.at[d],
            device_id={"tensor": to[d]},
            device_id_type=MESH,
        )

    def pass_on(d, c, k):
        slot = rs.at[d, k, c]
        rs_copy(d, c, k + 1, slot).wait_recv()
        here = rows_at(c, at_ring(p + sign[d] * k))
        if k + 1 == far:
            sender_cols = pl.ds(pl.multiple_of(at_ring(p - sign[d]) * cols, cols), cols)
            late = ex_in[d, pl.ds((c - d * n_chunk) * CHUNK, CHUNK), :].astype(F32)
            slot[:, sender_cols] = (slot[:, sender_cols].astype(F32) + late).astype(BF16)
        slot[...] = (slot[...].astype(F32) + partial[here, :].astype(F32)).astype(BF16)
        rs_copy(d, c, k, slot).start()

    for i in range(n_chunk):
        for d in range(2):
            begin(d, whole_way[d][i], far)

    run_pass(1)
    loads[2].wait()
    for k in range(1, T):
        dlow_copy(k, lax.rem(t + T - k, T)).wait_recv()

    def add_terms(block):
        term = jnp.dot(dlow[block], up[...], preferred_element_type=F32)
        at = pl.ds(row_of(block), share)
        partial[at, my_cols] = (partial[at, my_cols].astype(F32) + term).astype(BF16)

    term = jnp.dot(dlow[at_ring(p + far)], up[...], preferred_element_type=F32)
    ex_out[0] = term[:half].astype(BF16)
    ex_out[1] = term[half:].astype(BF16)
    for d in range(2):
        ex_copy(d).start()

    def terms_of(i):
        for block in pair(i):
            add_terms(block)

    terms_of(1)
    for i in range(n_chunk):
        for d in range(2):
            begin(d, one_less[d][i], far - 1)
    for d in range(2):
        ex_copy(d).wait_recv()
    for i in range(n_chunk):
        for d in range(2):
            pass_on(d, whole_way[d][i], far - 1)
    if far > 2:
        run_pass(2)
        terms_of(2)
    for k in range(far - 2, 0, -1):
        for i in range(all_chunks):
            if i == n_chunk and k > 1:
                run_pass(far - k + 1)
                terms_of(far - k + 1)
            for d in range(2):
                pass_on(d, (mixed if d == 0 or k == 1 else swapped)[i], k)
    add_terms(t)

    def sec_copy(c):
        return pltpu.make_async_remote_copy(
            src_ref=stream_ref.at[in_share(c)],
            dst_ref=arrived.at[in_share(c)],
            send_sem=sec_ss.at[c],
            recv_sem=sec_rs.at[c],
            device_id={"section": next_sec},
            device_id_type=MESH,
        )

    def ag_copy(d, c, hop, block):
        return pltpu.make_async_remote_copy(
            src_ref=ag.at[rows_at(c, block)],
            dst_ref=ag.at[rows_at(c, block)],
            send_sem=ag_ss.at[d, hop, c],
            recv_sem=ag_rs.at[d, hop, c],
            device_id={"tensor": to[d]},
            device_id_type=MESH,
        )

    loads[3].wait()

    def finish(c):
        at = in_share(c)
        total = partial[rows_at(c, t), :].astype(F32) + residual[at, :].astype(F32)
        for d in range(2):
            rs_copy(d, c, 1, rs.at[d, 0, c]).wait_recv()
            total = total + rs[d, 0, c].astype(F32)
        stream_ref[at, :] = total.astype(BF16)
        sec_copy(c).start()

    def normalise(c):
        sec_copy(c).wait_recv()
        values = arrived[in_share(c), :].astype(F32)
        inverse = lax.rsqrt(jnp.mean(values * values, axis=-1, keepdims=True) + 1e-05)
        ag[rows_at(c, t), :] = (values * inverse * gain_ref[...].astype(F32)).astype(BF16)
        for d in range(2):
            ag_copy(d, c, 0, t).start()

    for i, c in enumerate(mixed):
        finish(c)
        if i:
            normalise(mixed[i - 1])
    normalise(mixed[-1])

    for load in loads[4:]:
        load.wait()
    qlow[...] = jnp.zeros_like(qlow)

    NT = (((1,), (1,)), ((), ()))

    def multiply(blocks):
        count = len(blocks) * share
        for i, block in enumerate(blocks):
            lhs2[pl.ds(i * share, share), :] = ag[pl.ds(row_of(block), share), :]
        low = lax.dot_general(lhs2[:count], qshrink[...], NT, preferred_element_type=F32)
        for i, block in enumerate(blocks):
            qlow[pl.ds(row_of(block), share), :rc] = low[i * share : (i + 1) * share]

        def rest():
            got = jnp.dot(lhs2[:count], qkv_w[...], preferred_element_type=F32)
            for i, block in enumerate(blocks):
                acc[pl.ds(row_of(block), share), :] = got[i * share : (i + 1) * share]

        return rest

    multiply([t])()
    for hop in range(far - 1):
        for c in mixed:
            for d in range(2):
                block = at_ring(p - sign[d] * (hop + 1))
                ag_copy(d, c, hop, block).wait_recv()
                if hop + 1 < far - 1 or c in whole_way[d]:
                    ag_copy(d, c, hop + 1, block).start()
        multiply([at_ring(p - hop - 1), at_ring(p + hop + 1)])()
    opposite = at_ring(p + far)
    for d in range(2):
        for c in whole_way[d]:
            ag_copy(d, c, far - 1, opposite).wait_recv()
    rest = multiply([opposite])
    scale_copy.wait()
    qlow_all[t] = (qlow[...].T[:rc] * scale_t[...]).astype(BF16)

    def ql_copy(k, block):
        return pltpu.make_async_remote_copy(
            src_ref=qlow_all.at[block],
            dst_ref=qlow_all.at[block],
            send_sem=ql_ss.at[k],
            recv_sem=ql_rs.at[k],
            device_id={"tensor": lax.rem(t + k, T)},
            device_id_type=MESH,
        )

    for k in range(1, T):
        ql_copy(k, t).start()
    rest()
    for k in range(1, T):
        ql_copy(k, lax.rem(t + T - k, T)).wait_recv()
    small = qlow_all[...].reshape(T * rc, rows)
    for i in range(rows // 128):
        at = slice(i * 128, (i + 1) * 128)
        added = lax.dot_general(
            small[:, at], expand[...], (((0,), (0,)), ((), ())), preferred_element_type=F32
        )
        out_ref[at, :] = (acc[at, :] + added).astype(BF16)

    for k in range(1, T):
        low_copy(k).wait_send()
        dlow_copy(k, t).wait_send()
        ql_copy(k, t).wait_send()
    for c in range(all_chunks):
        sec_copy(c).wait_send()
    for d in range(2):
        ex_copy(d).wait_send()
        for c in range(all_chunks):
            for k in range(far - 1):
                rs_copy(d, c, k + 1, rs.at[d, k, c]).wait_send()
                ag_copy(d, c, k, t).wait_send()
        for i in range(n_chunk):
            ag_copy(d, whole_way[d][i], far - 1, t).wait_send()
            rs_copy(d, whole_way[d][i], far, rs.at[d, far - 1, 0]).wait_send()


def copy_out(stream_in, out_in, stream_ref, out_ref, sem):
    copies = []
    for source, target, size in ((out_in, out_ref, 64), (stream_in, stream_ref, CHUNK)):
        for first in range(0, source.shape[0], size):
            at = pl.ds(first, size)
            copies.append(
                pltpu.make_async_copy(source.at[at], target.at[at], sem.at[len(copies)])
            )
    for copy in copies:
        copy.start()
    for copy in copies:
        copy.wait()


def per_device(
    T,
    S,
    hidden,
    down_weight,
    down_shrink,
    down_up_factors,
    residual,
    tenant_ids,
    adapter_rank,
    adapter_offset,
    norm_gain,
    qkv_weight,
    qkv_shrink,
    qkv_expand,
):
    rows, K = hidden.shape
    D = residual.shape[1]
    share = rows // T
    half = share // 2
    R = down_shrink.shape[2]
    Q = qkv_weight.shape[2]
    rc = qkv_shrink.shape[2]
    cols = down_up_factors.shape[2]
    any_spec = pl.BlockSpec(memory_space=pl.ANY)
    vmem = pl.BlockSpec(memory_space=pltpu.VMEM)
    dma = pltpu.SemaphoreType.DMA
    smem = pl.BlockSpec(memory_space=pltpu.SMEM)
    outs = pl.pallas_call(
        functools.partial(kernel, T, S),
        out_shape=(
            pltpu.VMEM((share, D), BF16),
            pltpu.VMEM((rows, Q), BF16),
        ),
        in_specs=[any_spec] * 5 + [vmem] + [any_spec] * 3 + [vmem, smem, smem],
        out_specs=(vmem, vmem),
        scratch_shapes=[
            pltpu.VMEM((rows, K), BF16),
            pltpu.VMEM((K, D), BF16),
            pltpu.VMEM((K, R), BF16),
            pltpu.VMEM((R, cols), BF16),
            pltpu.VMEM((share, D), BF16),
            pltpu.VMEM((D, Q), BF16),
            pltpu.VMEM((rc, D), BF16),
            pltpu.VMEM((R, Q), BF16),
            pltpu.VMEM((rows, D), BF16),
            pltpu.VMEM((2 * share, K), BF16),
            pltpu.VMEM((T, share, R), BF16),
            pltpu.VMEM((T, share, R), BF16),
            pltpu.VMEM((T, share, R), BF16),
            pltpu.VMEM((2, half, cols), BF16),
            pltpu.VMEM((2, half, cols), BF16),
            pltpu.VMEM((2, T // 2, share // CHUNK, CHUNK, D), BF16),
            pltpu.VMEM((share, D), BF16),
            pltpu.VMEM((rc, rows), F32),
            pltpu.VMEM((R, rows), F32),
            pltpu.VMEM((rows, R), F32),
            pltpu.VMEM((rows, D), BF16),
            pltpu.VMEM((2 * share, D), BF16),
            pltpu.VMEM((rows, Q), F32),
            pltpu.VMEM((rows, 128), F32),
            pltpu.VMEM((T, rc, rows), BF16),
            dma((7,)),
            dma((D // WIDE,)),
            dma((T,)),
            dma((T,)),
            dma((T,)),
            dma((T,)),
            dma((2,)),
            dma((2,)),
            dma((2, T // 2, share // CHUNK)),
            dma((2, T // 2, share // CHUNK)),
            dma((share // CHUNK,)),
            dma((share // CHUNK,)),
            dma((1,)),
            dma((1,)),
            dma((2, T // 2, share // CHUNK)),
            dma((2, T // 2, share // CHUNK)),
            dma((T,)),
            dma((T,)),
        ],
        compiler_params=pltpu.CompilerParams(
            collective_id=0, has_side_effects=True, vmem_limit_bytes=61 * 1024 * 1024
        ),
        name="relay_boundary",
    )(
        hidden,
        down_weight[0],
        down_shrink[0],
        down_up_factors[0],
        residual,
        norm_gain,
        qkv_weight[0],
        qkv_shrink[0].T,
        qkv_expand[0],
        tenant_ids.reshape(1, rows),
        adapter_rank,
        adapter_offset,
    )
    return pl.pallas_call(
        copy_out,
        out_shape=tuple(jax.ShapeDtypeStruct(o.shape, o.dtype) for o in outs),
        in_specs=[any_spec] * 2,
        out_specs=(any_spec, any_spec),
        scratch_shapes=[dma((rows // 64 + share // CHUNK,))],
        name="copy_out",
    )(*outs)


def solution(mesh):
    in_specs = (
        P("section", "tensor"),
        P("section", "tensor", None),
        P("section", "tensor", None),
        P("section", None, "tensor"),
        P(("section", "tensor"), None),
        P("section"),
        P(),
        P(),
        P("section", None),
        P("section", None, "tensor"),
        P("section", None, "tensor"),
        P("section", None, "tensor"),
    )
    out_specs = (P(("section", "tensor"), None), P("section", "tensor"))
    body = functools.partial(per_device, mesh.shape["tensor"], mesh.shape["section"])
    return jax.shard_map(
        body, mesh=mesh, in_specs=in_specs, out_specs=out_specs, check_vma=False
    )
```

```python
import functools

import jax
import jax.numpy as jnp
from jax import lax
from jax.experimental import pallas as pl
from jax.experimental.pallas import tpu as pltpu
from jax.sharding import PartitionSpec as P

adapter_alpha_scale = 32.0
MESH = pl.DeviceIdType.MESH
F32 = jnp.float32
BF16 = jnp.bfloat16
CHUNK = 16
WIDE = 512


def kernel(
    T,
    S,
    hidden_in,
    down_in,
    shrink_in,
    up_in,
    residual_in,
    gain_ref,
    qkv_in,
    qshrink_in,
    expand_in,
    ids_ref,
    rank_ref,
    offset_ref,
    stream_ref,
    out_ref,
    hidden,
    down,
    shrink,
    up,
    residual,
    qkv_w,
    qshrink,
    expand,
    partial,
    lhs,
    low_mine,
    low_in,
    dlow,
    ex_out,
    ex_in,
    rs,
    arrived,
    scale_t,
    scale_all,
    scale_rows,
    ag,
    lhs2,
    acc,
    qlow,
    qlow_all,
    load_sem,
    down_sem,
    low_ss,
    low_rs,
    dlow_ss,
    dlow_rs,
    ex_ss,
    ex_rs,
    rs_ss,
    rs_rs,
    sec_ss,
    sec_rs,
    sc_ss,
    sc_rs,
    ag_ss,
    ag_rs,
    ql_ss,
    ql_rs,
):
    rows, D = partial.shape
    share = rows // T
    half = share // 2
    n_chunk = half // CHUNK
    cols = D // T
    rc = qshrink.shape[0]
    n_wide = D // WIDE
    t = lax.axis_index("tensor")
    sec = lax.axis_index("section")
    next_sec = lax.rem(sec + 1, S)
    prev_sec = lax.rem(sec + S - 1, S)
    h = t // 2
    p = h + lax.rem(t, 2) * (T - 1 - 2 * h)

    def at_ring(q):
        q = lax.rem(q + 2 * T, T)
        u = q // (T // 2)
        return (1 - u) * 2 * q + u * (2 * (T - 1 - q) + 1)

    to = (at_ring(p + 1), at_ring(p - 1))
    sign = (1, -1)
    far = T // 2
    all_chunks = 2 * n_chunk
    first_half, second_half = range(n_chunk), range(n_chunk, all_chunks)
    mixed = [c for pair_of in zip(second_half, first_half) for c in pair_of]
    swapped = [c for pair_of in zip(first_half, second_half) for c in pair_of]
    whole_way = (first_half, second_half)
    one_less = (second_half, first_half)

    loads = [
        pltpu.make_async_copy(a, b, load_sem.at[i])
        for i, (a, b) in enumerate(
            (
                (hidden_in, hidden),
                (shrink_in, shrink),
                (up_in, up),
                (residual_in, residual),
                (qkv_in, qkv_w),
                (qshrink_in, qshrink),
                (expand_in, expand),
            )
        )
    ]

    def down_load(j):
        at = pl.ds(pl.multiple_of(j * WIDE, WIDE), WIDE)
        return pltpu.make_async_copy(down_in.at[:, at], down.at[:, at], down_sem.at[j])

    loads[0].start()
    loads[1].start()
    for j in range(n_wide):
        down_load(j).start()
    for load in loads[2:]:
        load.start()

    barrier = pltpu.get_barrier_semaphore()
    for k in range(1, T):
        pl.semaphore_signal(
            barrier, inc=1, device_id={"tensor": lax.rem(t + k, T)}, device_id_type=MESH
        )
    for other in (next_sec, prev_sec):
        pl.semaphore_signal(
            barrier, inc=1, device_id={"section": other}, device_id_type=MESH
        )

    ids = ids_ref[...]
    lower = jnp.zeros_like(ids)
    ranks = jnp.zeros_like(ids)
    for k in range(rank_ref.shape[0]):
        lower = lower + jnp.where(ids == k, offset_ref[k], 0)
        ranks = ranks + jnp.where(ids == k, rank_ref[k], 0)
    column = lax.broadcasted_iota(jnp.int32, scale_all.shape, 0)
    inside = (column >= lower) & (column < lower + ranks)
    scale_all[...] = jnp.where(inside, adapter_alpha_scale / ranks.astype(F32), 0.0)
    scale_rows[...] = scale_all[...].T

    loads[0].wait()
    loads[1].wait()
    low_mine[...] = (
        jnp.dot(hidden[...], shrink[...], preferred_element_type=F32)
        .astype(BF16)
        .reshape(low_mine.shape)
    )
    pl.semaphore_wait(barrier, T + 1)

    def low_copy(k):
        peer = lax.rem(t + k, T)
        return pltpu.make_async_remote_copy(
            src_ref=low_mine.at[peer],
            dst_ref=low_in.at[k],
            send_sem=low_ss.at[k],
            recv_sem=low_rs.at[k],
            device_id={"tensor": peer},
            device_id_type=MESH,
        )

    def dlow_copy(k, block):
        return pltpu.make_async_remote_copy(
            src_ref=dlow.at[block],
            dst_ref=dlow.at[block],
            send_sem=dlow_ss.at[k],
            recv_sem=dlow_rs.at[k],
            device_id={"tensor": lax.rem(t + k, T)},
            device_id_type=MESH,
        )

    for k in range(1, T):
        low_copy(k).start()

    scale_copy = pltpu.make_async_remote_copy(
        src_ref=scale_all.at[pl.ds(pl.multiple_of(t * rc, rc), rc)],
        dst_ref=scale_t,
        send_sem=sc_ss.at[0],
        recv_sem=sc_rs.at[0],
        device_id={"section": next_sec},
        device_id_type=MESH,
    )
    scale_copy.start()

    def product(j, first, second):
        at = pl.ds(pl.multiple_of(j * WIDE, WIDE), WIDE)
        got = jnp.dot(lhs[...], down[:, at], preferred_element_type=F32).astype(BF16)
        partial[pl.ds(first, share), at] = got[:share]
        partial[pl.ds(second, share), at] = got[share:]

    def pair(i):
        return at_ring(p + far - i), (t if i == 0 else at_ring(p - far + i))

    def row_of(block):
        return pl.multiple_of(block * share, share)

    def fill(i):
        a, b = pair(i)
        lhs[:share] = hidden[pl.ds(row_of(a), share), :]
        lhs[share:] = hidden[pl.ds(row_of(b), share), :]
        return row_of(a), row_of(b)

    my_cols = pl.ds(pl.multiple_of(t * cols, cols), cols)

    def adapter_term(block):
        return jnp.dot(dlow[block], up[...], preferred_element_type=F32)

    def add_adapter(first, count, term):
        at = pl.ds(pl.multiple_of(first, CHUNK), count)
        partial[at, my_cols] = (partial[at, my_cols].astype(F32) + term).astype(BF16)

    def run_pass(i):
        first, second = fill(i)

        @pl.loop(0, n_wide)
        def _(j):
            product(j, first, second)

    first, second = fill(0)

    def early(j):
        down_load(j).wait()
        product(j, first, second)

    pl.loop(0, n_wide // 2)(early)
    total = low_mine[t].astype(F32)
    for k in range(1, T):
        low_copy(k).wait_recv()
        total = total + low_in[k].astype(F32)
    dlow[t] = (total * scale_rows[pl.ds(row_of(t), share), :]).astype(BF16)
    for k in range(1, T):
        dlow_copy(k, t).start()
    pl.loop(n_wide // 2, n_wide)(early)

    def rs_copy(d, c, k, src):
        return pltpu.make_async_remote_copy(
            src_ref=src,
            dst_ref=rs.at[d, k - 1, c],
            send_sem=rs_ss.at[d, k - 1, c],
            recv_sem=rs_rs.at[d, k - 1, c],
            device_id={"tensor": to[d]},
            device_id_type=MESH,
        )

    def rows_at(c, block):
        return pl.ds(pl.multiple_of(block * share + c * CHUNK, CHUNK), CHUNK)

    def in_share(c):
        return pl.ds(c * CHUNK, CHUNK)

    def begin(d, c, k):
        rs_copy(d, c, k, partial.at[rows_at(c, at_ring(p + sign[d] * k))]).start()

    def ex_copy(d):
        return pltpu.make_async_remote_copy(
            src_ref=ex_out.at[d],
            dst_ref=ex_in.at[d],
            send_sem=ex_ss.at[d],
            recv_sem=ex_rs.at[d],
            device_id={"tensor": to[d]},
            device_id_type=MESH,
        )

    def pass_on(d, c, k):
        slot = rs.at[d, k, c]
        rs_copy(d, c, k + 1, slot).wait_recv()
        here = rows_at(c, at_ring(p + sign[d] * k))
        if k + 1 == far:
            sender_cols = pl.ds(pl.multiple_of(at_ring(p - sign[d]) * cols, cols), cols)
            late = ex_in[d, pl.ds((c - d * n_chunk) * CHUNK, CHUNK), :].astype(F32)
            slot[:, sender_cols] = (slot[:, sender_cols].astype(F32) + late).astype(BF16)
        slot[...] = (slot[...].astype(F32) + partial[here, :].astype(F32)).astype(BF16)
        rs_copy(d, c, k, slot).start()

    for i in range(n_chunk):
        for d in range(2):
            begin(d, whole_way[d][i], far)

    run_pass(1)
    loads[2].wait()
    for k in range(1, T):
        dlow_copy(k, lax.rem(t + T - k, T)).wait_recv()

    def add_terms(block):
        term = jnp.dot(dlow[block], up[...], preferred_element_type=F32)
        at = pl.ds(row_of(block), share)
        partial[at, my_cols] = (partial[at, my_cols].astype(F32) + term).astype(BF16)

    term = jnp.dot(dlow[at_ring(p + far)], up[...], preferred_element_type=F32)
    ex_out[0] = term[:half].astype(BF16)
    ex_out[1] = term[half:].astype(BF16)
    for d in range(2):
        ex_copy(d).start()

    def terms_of(i):
        for block in pair(i):
            add_terms(block)

    terms_of(1)
    for i in range(n_chunk):
        for d in range(2):
            begin(d, one_less[d][i], far - 1)
    if far > 2:
        run_pass(2)
        terms_of(2)
    for d in range(2):
        ex_copy(d).wait_recv()
    for i in range(n_chunk):
        for d in range(2):
            pass_on(d, whole_way[d][i], far - 1)
    for k in range(far - 2, 0, -1):
        if far - k > 2:
            run_pass(far - k)
            terms_of(far - k)
        for i in range(all_chunks):
            for d in range(2):
                pass_on(d, (mixed if d == 0 or k == 1 else swapped)[i], k)
    add_terms(t)

    def sec_copy(c):
        return pltpu.make_async_remote_copy(
            src_ref=stream_ref.at[in_share(c)],
            dst_ref=arrived.at[in_share(c)],
            send_sem=sec_ss.at[c],
            recv_sem=sec_rs.at[c],
            device_id={"section": next_sec},
            device_id_type=MESH,
        )

    def ag_copy(d, c, hop, block):
        return pltpu.make_async_remote_copy(
            src_ref=ag.at[rows_at(c, block)],
            dst_ref=ag.at[rows_at(c, block)],
            send_sem=ag_ss.at[d, hop, c],
            recv_sem=ag_rs.at[d, hop, c],
            device_id={"tensor": to[d]},
            device_id_type=MESH,
        )

    loads[3].wait()

    def finish(c):
        at = in_share(c)
        total = partial[rows_at(c, t), :].astype(F32) + residual[at, :].astype(F32)
        for d in range(2):
            rs_copy(d, c, 1, rs.at[d, 0, c]).wait_recv()
            total = total + rs[d, 0, c].astype(F32)
        stream_ref[at, :] = total.astype(BF16)
        sec_copy(c).start()

    def normalise(c):
        sec_copy(c).wait_recv()
        values = arrived[in_share(c), :].astype(F32)
        inverse = lax.rsqrt(jnp.mean(values * values, axis=-1, keepdims=True) + 1e-05)
        ag[rows_at(c, t), :] = (values * inverse * gain_ref[...].astype(F32)).astype(BF16)
        for d in range(2):
            ag_copy(d, c, 0, t).start()

    for i, c in enumerate(mixed):
        finish(c)
        if i:
            normalise(mixed[i - 1])
    normalise(mixed[-1])

    for load in loads[4:]:
        load.wait()
    qlow[...] = jnp.zeros_like(qlow)

    NT = (((1,), (1,)), ((), ()))

    def multiply(blocks):
        count = len(blocks) * share
        for i, block in enumerate(blocks):
            lhs2[pl.ds(i * share, share), :] = ag[pl.ds(row_of(block), share), :]
        low = lax.dot_general(lhs2[:count], qshrink[...], NT, preferred_element_type=F32)
        for i, block in enumerate(blocks):
            qlow[pl.ds(row_of(block), share), :rc] = low[i * share : (i + 1) * share]

        def rest():
            got = jnp.dot(lhs2[:count], qkv_w[...], preferred_element_type=F32)
            for i, block in enumerate(blocks):
                acc[pl.ds(row_of(block), share), :] = got[i * share : (i + 1) * share]

        return rest

    multiply([t])()
    for hop in range(far - 1):
        for c in mixed:
            for d in range(2):
                block = at_ring(p - sign[d] * (hop + 1))
                ag_copy(d, c, hop, block).wait_recv()
                if hop + 1 < far - 1 or c in whole_way[d]:
                    ag_copy(d, c, hop + 1, block).start()
        multiply([at_ring(p - hop - 1), at_ring(p + hop + 1)])()
    opposite = at_ring(p + far)
    for d in range(2):
        for c in whole_way[d]:
            ag_copy(d, c, far - 1, opposite).wait_recv()
    rest = multiply([opposite])
    scale_copy.wait()
    qlow_all[t] = (qlow[...].T[:rc] * scale_t[...]).astype(BF16)

    def ql_copy(k, block):
        return pltpu.make_async_remote_copy(
            src_ref=qlow_all.at[block],
            dst_ref=qlow_all.at[block],
            send_sem=ql_ss.at[k],
            recv_sem=ql_rs.at[k],
            device_id={"tensor": lax.rem(t + k, T)},
            device_id_type=MESH,
        )

    for k in range(1, T):
        ql_copy(k, t).start()
    rest()
    for k in range(1, T):
        ql_copy(k, lax.rem(t + T - k, T)).wait_recv()
    small = qlow_all[...].reshape(T * rc, rows)
    added = lax.dot_general(
        small, expand[...], (((0,), (0,)), ((), ())), preferred_element_type=F32
    )
    out_ref[...] = (acc[...] + added).astype(BF16)

    for k in range(1, T):
        low_copy(k).wait_send()
        dlow_copy(k, t).wait_send()
        ql_copy(k, t).wait_send()
    for c in range(all_chunks):
        sec_copy(c).wait_send()
    for d in range(2):
        ex_copy(d).wait_send()
        for c in range(all_chunks):
            for k in range(far if c in whole_way[d] else far - 1):
                rs_copy(d, c, k + 1, rs.at[d, k, c]).wait_send()
                ag_copy(d, c, k, t).wait_send()


def copy_out(stream_in, out_in, stream_ref, out_ref, stream, out, in_sem, out_sem):
    reads, writes = [], []
    for source, held, target, size in (
        (out_in, out, out_ref, 64),
        (stream_in, stream, stream_ref, CHUNK),
    ):
        for first in range(0, source.shape[0], size):
            at, i = pl.ds(first, size), len(reads)
            reads.append(pltpu.make_async_copy(source.at[at], held.at[at], in_sem.at[i]))
            writes.append(pltpu.make_async_copy(held.at[at], target.at[at], out_sem.at[i]))
    for read in reads:
        read.start()
    for read, write in zip(reads, writes):
        read.wait()
        write.start()
    for write in writes:
        write.wait()


def per_device(
    T,
    S,
    hidden,
    down_weight,
    down_shrink,
    down_up_factors,
    residual,
    tenant_ids,
    adapter_rank,
    adapter_offset,
    norm_gain,
    qkv_weight,
    qkv_shrink,
    qkv_expand,
):
    rows, K = hidden.shape
    D = residual.shape[1]
    share = rows // T
    half = share // 2
    R = down_shrink.shape[2]
    Q = qkv_weight.shape[2]
    rc = qkv_shrink.shape[2]
    cols = down_up_factors.shape[2]
    any_spec = pl.BlockSpec(memory_space=pl.ANY)
    vmem = pl.BlockSpec(memory_space=pltpu.VMEM)
    dma = pltpu.SemaphoreType.DMA
    smem = pl.BlockSpec(memory_space=pltpu.SMEM)
    outs = pl.pallas_call(
        functools.partial(kernel, T, S),
        out_shape=(
            jax.ShapeDtypeStruct((share, D), BF16),
            jax.ShapeDtypeStruct((rows, Q), BF16),
        ),
        in_specs=[any_spec] * 5 + [vmem] + [any_spec] * 3 + [vmem, smem, smem],
        out_specs=(vmem, vmem),
        scratch_shapes=[
            pltpu.VMEM((rows, K), BF16),
            pltpu.VMEM((K, D), BF16),
            pltpu.VMEM((K, R), BF16),
            pltpu.VMEM((R, cols), BF16),
            pltpu.VMEM((share, D), BF16),
            pltpu.VMEM((D, Q), BF16),
            pltpu.VMEM((rc, D), BF16),
            pltpu.VMEM((R, Q), BF16),
            pltpu.VMEM((rows, D), BF16),
            pltpu.VMEM((2 * share, K), BF16),
            pltpu.VMEM((T, share, R), BF16),
            pltpu.VMEM((T, share, R), BF16),
            pltpu.VMEM((T, share, R), BF16),
            pltpu.VMEM((2, half, cols), BF16),
            pltpu.VMEM((2, half, cols), BF16),
            pltpu.VMEM((2, T // 2, share // CHUNK, CHUNK, D), BF16),
            pltpu.VMEM((share, D), BF16),
            pltpu.VMEM((rc, rows), F32),
            pltpu.VMEM((R, rows), F32),
            pltpu.VMEM((rows, R), F32),
            pltpu.VMEM((rows, D), BF16),
            pltpu.VMEM((2 * share, D), BF16),
            pltpu.VMEM((rows, Q), F32),
            pltpu.VMEM((rows, 128), F32),
            pltpu.VMEM((T, rc, rows), BF16),
            dma((7,)),
            dma((D // WIDE,)),
            dma((T,)),
            dma((T,)),
            dma((T,)),
            dma((T,)),
            dma((2,)),
            dma((2,)),
            dma((2, T // 2, share // CHUNK)),
            dma((2, T // 2, share // CHUNK)),
            dma((share // CHUNK,)),
            dma((share // CHUNK,)),
            dma((1,)),
            dma((1,)),
            dma((2, T // 2, share // CHUNK)),
            dma((2, T // 2, share // CHUNK)),
            dma((T,)),
            dma((T,)),
        ],
        compiler_params=pltpu.CompilerParams(
            collective_id=0, has_side_effects=True, vmem_limit_bytes=61 * 1024 * 1024
        ),
        name="relay_boundary",
    )(
        hidden,
        down_weight[0],
        down_shrink[0],
        down_up_factors[0],
        residual,
        norm_gain,
        qkv_weight[0],
        qkv_shrink[0].T,
        qkv_expand[0],
        tenant_ids.reshape(1, rows),
        adapter_rank,
        adapter_offset,
    )
    return pl.pallas_call(
        copy_out,
        out_shape=tuple(jax.ShapeDtypeStruct(o.shape, o.dtype) for o in outs),
        in_specs=[any_spec] * 2,
        out_specs=(any_spec, any_spec),
        scratch_shapes=[
            pltpu.VMEM((share, D), BF16),
            pltpu.VMEM((rows, Q), BF16),
            dma((rows // 64 + share // CHUNK,)),
            dma((rows // 64 + share // CHUNK,)),
        ],
        compiler_params=pltpu.CompilerParams(vmem_limit_bytes=61 * 1024 * 1024),
        name="copy_out",
    )(*outs)


def solution(mesh):
    in_specs = (
        P("section", "tensor"),
        P("section", "tensor", None),
        P("section", "tensor", None),
        P("section", None, "tensor"),
        P(("section", "tensor"), None),
        P("section"),
        P(),
        P(),
        P("section", None),
        P("section", None, "tensor"),
        P("section", None, "tensor"),
        P("section", None, "tensor"),
    )
    out_specs = (P(("section", "tensor"), None), P("section", "tensor"))
    body = functools.partial(per_device, mesh.shape["tensor"], mesh.shape["section"])
    return jax.shard_map(
        body, mesh=mesh, in_specs=in_specs, out_specs=out_specs, check_vma=False
    )
```
